32 devices in a mesh: gx: 2 (over x), gy: 4 (over z), gz: 4 (over y, core).
Axes of the slice: x: 2, y: 2, z: 4, core: 2. Of those that a mesh axis runs over, the one named last changes fastest.
Arguments:
- fields: float32 [5, 64, 256, 512], P(None, 'gx', 'gy', 'gz'), may hold values from -4 to 9
- viscous: float32 [5], replicated, may hold values from 1 to 8000
Outputs:
- updated: float32 [5, 64, 256, 512], P(None, 'gx', 'gy', 'gz')
The draws below stay inside these ranges and needn't reach their ends.
All inputs are finite; a program needn't handle non-finite values.
Results may differ from the reference program's by a relative error of at most 0.0003.
Values sent between devices are 32-bit elements; how exact they have to be, the bound alone decides.
A program may use at most 128 MiB of HBM per device.

```python
import math
import jax
import jax.numpy as jnp
from jax import lax

NF = 5
NX = 64
NY = 256
NZ = 512


def draw_fields(key, part):
    keys = jax.random.split(jax.random.fold_in(key, 7), 7)
    height = (jnp.arange(NY, dtype=jnp.float32) + 0.5) / NY
    profile = 4.0 * height * (1.0 - height)
    amplitude = jax.random.uniform(keys[0], (NF,), jnp.float32, 0.5, 1.5)
    amplitude = jnp.where(jnp.arange(NF) == 0, amplitude + 4.5, amplitude)
    total = amplitude[:, None, None, None] * profile[None, None, :, None]
    mode_count = 3
    lowest_wave = 3 * NX // 10
    highest_wave = 2 * NX // 5 + 1
    wave_number = jax.random.randint(keys[1], (NF, mode_count), lowest_wave, highest_wave)
    height_wave = jax.random.randint(keys[2], (NF, mode_count), 1, 4)
    height_phase = jax.random.uniform(keys[3], (NF, mode_count), jnp.float32, 0.0, 2.0 * math.pi)
    span_phase = jax.random.uniform(keys[4], (NF, mode_count, NZ), jnp.float32, 0.0, 2.0 * math.pi)
    mode_size = jax.random.uniform(keys[5], (NF, mode_count, NZ), jnp.float32, 0.6, 1.0)
    white = 0.3 * jax.random.normal(keys[6], (NF, NX, NY, NZ), jnp.float32)
    cells = jnp.arange(NX, dtype=jnp.int32)
    rows = jnp.arange(NY, dtype=jnp.int32)
    for mode in range(mode_count):
        turn = jnp.mod(wave_number[:, mode][:, None] * cells[None, :], NX).astype(jnp.float32) * (2.0 * math.pi / NX)
        height_turn = jnp.mod(height_wave[:, mode][:, None] * rows[None, :], NY).astype(jnp.float32) * (2.0 * math.pi / NY)
        envelope = 0.75 + 0.25 * jnp.cos(height_turn + height_phase[:, mode][:, None])
        wave = mode_size[:, mode][:, None, :] * jnp.sin(turn[:, :, None] + span_phase[:, mode][:, None, :])
        total = total + wave[:, :, None, :] * envelope[:, None, :, None]
    return jnp.clip(total + white, -4.0, 9.0)


def draw_viscous(key, part):
    keys = jax.random.split(jax.random.fold_in(key, 13), 3)
    rates = jnp.exp(jax.random.uniform(keys[0], (NF,), jnp.float32, 0.0, math.log(8000.0)))
    pick = jax.random.randint(keys[1], (), 0, NF)
    slots = jnp.arange(NF, dtype=jnp.int32)
    low_rate = jax.random.uniform(keys[2], (), jnp.float32, 1.0, 2.0)
    return jnp.where(slots == pick, low_rate, rates)


def setup_inputs(seed: int = 0) -> dict:
    streams_of = jax.random.split(jax.random.key(seed), 3)
    fields = draw_fields(jax.random.fold_in(streams_of[2], 71), 0)
    viscous = draw_viscous(jax.random.fold_in(streams_of[2], 71), 0)
    return {"fields": fields, "viscous": viscous}


advect = 0.3


def compact_slope(field):
    wave = 2.0 * math.pi * jnp.arange(NX // 2 + 1, dtype=jnp.float32) / NX
    symbol = (14.0 / 9.0 * jnp.sin(wave) + jnp.sin(2.0 * wave) / 18.0) / (1.0 + 2.0 / 3.0 * jnp.cos(wave))
    spectrum = jnp.fft.rfft(field, axis=0)
    return jnp.fft.irfft(spectrum * (1j * symbol)[:, None, None], n=NX, axis=0).astype(field.dtype)


def span_slope(field):
    def shifted(offset):
        return jnp.roll(field, -offset, axis=2)
    return (45.0 * (shifted(1) - shifted(-1)) - 9.0 * (shifted(2) - shifted(-2)) + (shifted(3) - shifted(-3))) / 60.0


def wall_solve(explicit, viscous):
    diagonal = 1.0 + 2.0 * viscous
    columns = jnp.moveaxis(explicit, 1, 0)

    def forward(carry, row_values):
        previous, eliminated = carry
        current = 1.0 / (diagonal - viscous * viscous * previous)
        eliminated = current * (row_values + viscous * eliminated)
        return (current, eliminated), (current, eliminated)

    start = (jnp.zeros((), explicit.dtype), jnp.zeros_like(columns[0]))
    _, (pivots, eliminated) = lax.scan(forward, start, columns)

    def backward(solved, pair):
        pivot, value = pair
        solved = value + viscous * pivot * solved
        return solved, solved

    _, solution = lax.scan(backward, jnp.zeros_like(columns[0]), (pivots, eliminated), reverse=True)
    return jnp.moveaxis(solution, 0, 1)


def reference(fields, viscous):
    along_velocity = fields[0]
    across_velocity = fields[2]

    def one_field(pair):
        field, rate = pair
        explicit = field - advect * along_velocity * compact_slope(field) - advect * across_velocity * span_slope(field)
        return wall_solve(explicit, rate)

    return lax.map(one_field, (fields, viscous))
```

```python
import functools
import math

import jax
import jax.numpy as jnp
from jax import lax
from jax.experimental import pallas as pl
from jax.experimental.pallas import tpu as pltpu
from jax.sharding import PartitionSpec as P

advect = 0.3
ratio = (-1.0 + math.sqrt(5.0) / 3.0) * 1.5
line_scale = -25.0 / 12.0
near_scale = 1.0 / 12.0
MESH = pl.DeviceIdType.MESH
f32 = jnp.float32
bf16 = jnp.bfloat16
GROUP = 4


def power(theta, count):
    return jnp.exp(-theta * count)


def rest(theta, count):
    return 1.0 - jnp.exp(-2.0 * theta * count)


def wall_tables(nu, place, rows, total, gm, tables, decay, f):
    shape = (rows + 16, 3 * rows)

    def theta_of(shape):
        half = 0.5 * lax.rsqrt(jnp.full(shape, nu, f32))
        return 2.0 * jnp.log(half + jnp.sqrt(1.0 + half * half))

    def scale_of(shape):
        theta = theta_of(shape)
        return power(theta, 1.0) / (nu * rest(theta, 1.0) * rest(theta, total + 1.0))

    theta = theta_of(shape)
    row = lax.broadcasted_iota(jnp.int32, shape, 0)
    lane = lax.broadcasted_iota(jnp.int32, shape, 1)
    col = jnp.bitwise_and(lane, rows - 1)
    start = place * rows
    low = (jnp.minimum(row, col) + start).astype(f32)
    high = (jnp.maximum(row, col) + start).astype(f32)
    own = (col + start).astype(f32)
    inner = scale_of(shape) * power(theta, high - low) * rest(theta, low + 1.0) * rest(theta, total - high)
    up = power(theta, (rows - col).astype(f32)) * rest(theta, own + 1.0)
    down = power(theta, (col + 1).astype(f32)) * rest(theta, total - own)
    full = jnp.where(row < rows, inner, jnp.where(row == rows, up, jnp.where(row == rows + 1, down, 0.0)))
    top = full.astype(bf16).astype(f32)
    gm[f] = jnp.where(lane >= 2 * rows, full - top, top).astype(bf16)

    shape = (rows, 128)
    theta = theta_of(shape)
    scale = scale_of(shape)
    row = lax.broadcasted_iota(jnp.int32, shape, 0)
    here = (row + start).astype(f32)
    tables[f, 0] = scale * power(theta, row.astype(f32)) * rest(theta, total - here)
    tables[f, 1] = scale * power(theta, (rows - 1 - row).astype(f32)) * rest(theta, here + 1.0)
    decay[f] = power(theta_of((8, 128)), float(rows))


def main_kernel(
    sizes, fields, viscous, v_out, t_out, c_out,
    q, e, xs, xr, zs, zr, ws, wr, gm, tables, decay, carry, merged,
    in_sem, out_sem, x_send, x_recv, z_send, z_recv, w_send, w_recv,
):
    px, py, pz = sizes
    nf, nx, ny, nz = q.shape
    blocks = nx // 32
    ix, iy, iz = lax.axis_index("gx"), lax.axis_index("gy"), lax.axis_index("gz")

    def x_at(k):
        return lax.rem(ix + k, px)

    z_up, z_down = lax.rem(iz + 1, pz), lax.rem(iz + pz - 1, pz)

    def load(f):
        return pltpu.make_async_copy(fields.at[f], q.at[f], in_sem.at[f])

    for f in range(nf):
        load(f).start()

    wr[...] = jnp.zeros_like(wr)
    barrier = pltpu.get_barrier_semaphore()
    for k in range(1, px):
        pl.semaphore_signal(barrier, inc=1, device_id={"gx": x_at(k)}, device_id_type=MESH)
    for to in (z_up, z_down):
        pl.semaphore_signal(barrier, inc=1, device_id={"gz": to}, device_id_type=MESH)
    for k in range(1, py):
        pl.semaphore_signal(barrier, inc=1, device_id={"gy": lax.rem(iy + k, py)}, device_id_type=MESH)

    def x_copy(f, k):
        return pltpu.make_async_remote_copy(
            src_ref=xs.at[f], dst_ref=xr.at[k - 1, f], send_sem=x_send.at[k - 1, f], recv_sem=x_recv.at[k - 1, f],
            device_id={"gx": x_at(k)}, device_id_type=MESH)

    def z_copy(f, side):
        return pltpu.make_async_remote_copy(
            src_ref=zs.at[side, f], dst_ref=zr.at[side, f], send_sem=z_send.at[side, f], recv_sem=z_recv.at[side, f],
            device_id={"gz": z_up if side == 0 else z_down}, device_id_type=MESH)

    def w_copy(f, side, k):
        to = lax.rem(iy + (k if side == 0 else py - k), py)
        return pltpu.make_async_remote_copy(
            src_ref=ws.at[side, f], dst_ref=wr.at[side, k - 1, f], send_sem=w_send.at[side, k - 1, f],
            recv_sem=w_recv.at[side, k - 1, f], device_id={"gy": to}, device_id_type=MESH)

    lane = lax.broadcasted_iota(jnp.int32, (ny, nz), 1)
    group = lax.shift_right_logical(lane, 2)
    zero = jnp.zeros((ny, nz), f32)

    def first_part(f, _):
        load(f).wait()

        def sums(t, state):
            fo, bo = state
            fo = ratio * (q[f, t] + fo)
            back = nx - 1 - t
            e[f, back] = bo
            bo = ratio * (q[f, back] + bo)
            return fo, bo

        fo, bo = lax.fori_loop(0, nx, sums, (zero, zero), unroll=2)
        xs[f, 0] = fo
        xs[f, 1] = q[f, nx - 1]
        xs[f, 2] = bo
        xs[f, 3] = q[f, 0]

        @pl.when(f == 0)
        def _():
            pl.semaphore_wait(barrier, px - 1 + 2 + py - 1)

        for k in range(1, px):
            x_copy(f, k).start()

        for g in range(blocks):
            def pack(t, state):
                last, lead = state
                turned = pltpu.roll(q[f, g * 32 + t], GROUP * t, 1)
                lead = jnp.where(group == t, turned, lead)
                last = jnp.where(group == jnp.bitwise_and(t + 31, 31), turned, last)
                return last, lead

            last, lead = lax.fori_loop(0, 32, pack, (zero, zero), unroll=2)
            zs[0, f, g] = last
            zs[1, f, g] = lead
        for side in range(2):
            z_copy(f, side).start()
        return 0

    lax.fori_loop(0, nf, first_part, 0)

    def build(f, _):
        wall_tables(viscous[f], iy, ny, ny * py, gm, tables, decay, f)
        return 0

    lax.fori_loop(0, nf, build, 0)
    t_copy = pltpu.make_async_copy(tables, t_out, out_sem.at[nf])
    t_copy.start()

    def second_part(f, _):
        def one(x, before):
            here = q[f, x]
            forward, previous = before
            after = jnp.where(x == nx - 1, 0.0, 1.0) * q[f, jnp.minimum(x + 1, nx - 1)]
            slope = line_scale * (e[f, x] - forward) + near_scale * (after - previous)

            def shifted(k):
                return pltpu.roll(here, (nz - k) % nz, 1)

            span = (
                0.75 * (shifted(1) - shifted(-1))
                - 0.15 * (shifted(2) - shifted(-2))
                + (1.0 / 60.0) * (shifted(3) - shifted(-3))
            )
            e[f, x] = here - advect * (q[0, x] * slope + q[2, x] * span)
            return ratio * (here + forward), here

        lax.fori_loop(0, nx, one, (zero, zero))
        return 0

    lax.fori_loop(0, nf, second_part, 0)

    inside = jnp.bitwise_and(lane, 3)
    even = jnp.bitwise_and(group, 1) == 0
    edges = jnp.logical_or(group == 0, group == nz // GROUP - 1)
    closing = 1.0 / (1.0 - ratio ** (nx * px))

    def third_part(f, _):
        for side in range(2):
            z_copy(f, side).wait_recv()
        for g in range(blocks):
            left = (zr[0, f, g] - zs[0, f, g]) * (1.0 / 60.0)
            right = (zr[1, f, g] - zs[1, f, g]) * (1.0 / 60.0)
            low = (
                jnp.where(inside == 0, -45.0 * pltpu.roll(left, nz - 3, 1), 0.0)
                + jnp.where(inside <= 1, 9.0 * pltpu.roll(left, nz - 2, 1), 0.0)
                - jnp.where(inside <= 2, pltpu.roll(left, nz - 1, 1), 0.0)
            )
            high = (
                jnp.where(inside == 3, 45.0 * pltpu.roll(right, 3, 1), 0.0)
                - jnp.where(inside >= 2, 9.0 * pltpu.roll(right, 2, 1), 0.0)
                + jnp.where(inside >= 1, pltpu.roll(right, 1, 1), 0.0)
            )
            low = pltpu.roll(low, GROUP, 1)
            high = pltpu.roll(high, nz - GROUP, 1)
            merged[g, 0] = jnp.where(even, low, high)
            merged[g, 1] = jnp.where(even, high, low)

        for k in range(1, px):
            x_copy(f, k).wait_recv()
        ahead = ratio ** (nx * (px - 1)) * xs[f, 0]
        behind = ratio ** (nx * (px - 1)) * xs[f, 2]
        for k in range(1, px):
            ahead = ahead + ratio ** (nx * (k - 1)) * xr[k - 1, f, 0]
            behind = behind + ratio ** (nx * (k - 1)) * xr[px - k - 1, f, 2]
        carry[0] = (advect * line_scale * closing) * ahead
        carry[1] = (-advect * line_scale * closing) * behind
        e[f, 0] = e[f, 0] + (advect * near_scale) * q[0, 0] * xr[0, f, 1]
        e[f, nx - 1] = e[f, nx - 1] - (advect * near_scale) * q[0, nx - 1] * xr[px - 2, f, 3]
        matrix = gm[f]

        for g in range(blocks):
            def pair(t, weights):
                fw, bw = weights
                tops, lows = [], []
                for o in range(2):
                    x = g * 32 + 2 * t + o
                    turned = pltpu.roll(merged[g, o], jnp.bitwise_and(nz - GROUP * (2 * t + o), nz - 1), 1)
                    span = jnp.where(edges, turned, 0.0)
                    whole = e[f, x] + q[0, x] * (fw * carry[0] + bw * carry[1]) - advect * q[2, x] * span
                    top = whole.astype(bf16)
                    tops.append(top)
                    lows.append((whole - top.astype(f32)).astype(bf16))
                    fw = fw * ratio
                    bw = bw * (1.0 / ratio)
                top = jnp.concatenate(tops, axis=1)
                right = jnp.concatenate([top, jnp.concatenate(lows, axis=1), top], axis=0)
                solved = jnp.dot(matrix, right, preferred_element_type=f32)
                for o in range(2):
                    x = g * 32 + 2 * t + o
                    e[f, x] = solved[:ny, o * nz : (o + 1) * nz]
                    ws[0, f, pl.ds(x, 1), :] = solved[ny : ny + 1, o * nz : (o + 1) * nz]
                    ws[1, f, pl.ds(x, 1), :] = solved[ny + 1 : ny + 2, o * nz : (o + 1) * nz]
                return fw, bw

            first = (f32(ratio ** (32 * g)), f32(ratio ** (nx - 1 - 32 * g)))
            lax.fori_loop(0, 16, pair, first)

        for k in range(1, py):
            @pl.when(iy + k < py)
            def _():
                w_copy(f, 0, k).start()

            @pl.when(iy >= k)
            def _():
                w_copy(f, 1, k).start()
        pltpu.make_async_copy(e.at[f], v_out.at[f], out_sem.at[f]).start()
        return 0

    lax.fori_loop(0, nf, third_part, 0)

    def fourth_part(f, _):
        for k in range(1, py):
            @pl.when(iy >= k)
            def _():
                w_copy(f, 0, k).wait_recv()

            @pl.when(iy + k < py)
            def _():
                w_copy(f, 1, k).wait_recv()
        step = jnp.broadcast_to(decay[f][0:1, :], (nx, nz))
        for side in range(2):
            total = wr[side, py - 2, f]
            for k in range(py - 2, 0, -1):
                total = wr[side, k - 1, f] + step * total
            c_out[side, f] = total
        return 0

    lax.fori_loop(0, nf, fourth_part, 0)

    def finish(f, _):
        for k in range(1, px):
            x_copy(f, k).wait_send()
        for side in range(2):
            z_copy(f, side).wait_send()
        for k in range(1, py):
            @pl.when(iy + k < py)
            def _():
                w_copy(f, 0, k).wait_send()

            @pl.when(iy >= k)
            def _():
                w_copy(f, 1, k).wait_send()
        pltpu.make_async_copy(e.at[f], v_out.at[f], out_sem.at[f]).wait()
        return 0

    lax.fori_loop(0, nf, finish, 0)
    t_copy.wait()


def last_kernel(v, tables, rows, out):
    for o in range(v.shape[1]):
        out[0, o] = (
            v[0, o]
            + tables[0, 0] * rows[0, 0, o : o + 1, :]
            + tables[0, 1] * rows[1, 0, o : o + 1, :]
        )


def shards(fields, viscous):
    nf, nx, ny, nz = fields.shape
    px, py, pz = (lax.axis_size(a) for a in ("gx", "gy", "gz"))
    blocks = nx // 32
    any_space = pl.BlockSpec(memory_space=pl.ANY)
    v, tables, rows = pl.pallas_call(
        functools.partial(main_kernel, (px, py, pz)),
        out_shape=(
            jax.ShapeDtypeStruct((nf, nx, ny, nz), f32),
            jax.ShapeDtypeStruct((nf, 2, ny, nz), f32),
            jax.ShapeDtypeStruct((2, nf, nx, nz), f32),
        ),
        in_specs=[any_space, pl.BlockSpec(memory_space=pltpu.SMEM)],
        out_specs=(any_space, any_space, pl.BlockSpec(memory_space=pltpu.VMEM)),
        scratch_shapes=[
            pltpu.VMEM((nf, nx, ny, nz), f32),
            pltpu.VMEM((nf, nx, ny, nz), f32),
            pltpu.VMEM((nf, 4, ny, nz), f32),
            pltpu.VMEM((px - 1, nf, 4, ny, nz), f32),
            pltpu.VMEM((2, nf, blocks, ny, nz), f32),
            pltpu.VMEM((2, nf, blocks, ny, nz), f32),
            pltpu.VMEM((2, nf, nx, nz), f32),
            pltpu.VMEM((2, py - 1, nf, nx, nz), f32),
            pltpu.VMEM((nf, ny + 16, 3 * ny), bf16),
            pltpu.VMEM((nf, 2, ny, nz), f32),
            pltpu.VMEM((nf, 8, nz), f32),
            pltpu.VMEM((2, ny, nz), f32),
            pltpu.VMEM((blocks, 2, ny, nz), f32),
            pltpu.SemaphoreType.DMA((nf,)),
            pltpu.SemaphoreType.DMA((nf + 1,)),
            pltpu.SemaphoreType.DMA((px - 1, nf)),
            pltpu.SemaphoreType.DMA((px - 1, nf)),
            pltpu.SemaphoreType.DMA((2, nf)),
            pltpu.SemaphoreType.DMA((2, nf)),
            pltpu.SemaphoreType.DMA((2, py - 1, nf)),
            pltpu.SemaphoreType.DMA((2, py - 1, nf)),
        ],
        compiler_params=pltpu.CompilerParams(
            collective_id=0, has_side_effects=True, vmem_limit_bytes=50 * 1024 * 1024
        ),
        name="section",
    )(fields, viscous)
    chunk = 16
    return pl.pallas_call(
        last_kernel,
        grid=(nf, nx // chunk),
        out_shape=jax.ShapeDtypeStruct((nf, nx, ny, nz), f32),
        in_specs=[
            pl.BlockSpec((1, chunk, ny, nz), lambda f, x: (f, x, 0, 0)),
            pl.BlockSpec((1, 2, ny, nz), lambda f, x: (f, 0, 0, 0)),
            pl.BlockSpec((2, 1, chunk, nz), lambda f, x: (0, f, x, 0)),
        ],
        out_specs=pl.BlockSpec((1, chunk, ny, nz), lambda f, x: (f, x, 0, 0)),
        compiler_params=pltpu.CompilerParams(vmem_limit_bytes=16 * 1024 * 1024),
        name="carried",
    )(v, tables, rows)


def solution(mesh):
    in_specs = (P(None, "gx", "gy", "gz"), P())
    out_specs = P(None, "gx", "gy", "gz")
    return jax.shard_map(shards, mesh=mesh, in_specs=in_specs, out_specs=out_specs, check_vma=False)
```

```python
import functools
import math

import jax
import jax.numpy as jnp
from jax import lax
from jax.experimental import pallas as pl
from jax.experimental.pallas import tpu as pltpu
from jax.sharding import PartitionSpec as P

advect = 0.3
ratio = (-1.0 + math.sqrt(5.0) / 3.0) * 1.5
line_scale = -25.0 / 12.0
near_scale = 1.0 / 12.0
MESH = pl.DeviceIdType.MESH
f32 = jnp.float32
bf16 = jnp.bfloat16
GROUP = 4
STEP = 8
SPAN_STEP = 8
PART = 8


def power(theta, count):
    return jnp.exp(-theta * count)


def rest(theta, count):
    return 1.0 - jnp.exp(-2.0 * theta * count)


def wall_tables(nu, place, rows, total, gm, tables, decay, f):
    shape = (rows + 16, 3 * rows)

    def theta_of(shape):
        half = 0.5 * lax.rsqrt(jnp.full(shape, nu, f32))
        return 2.0 * jnp.log(half + jnp.sqrt(1.0 + half * half))

    def scale_of(shape):
        theta = theta_of(shape)
        return power(theta, 1.0) / (nu * rest(theta, 1.0) * rest(theta, total + 1.0))

    theta = theta_of(shape)
    row = lax.broadcasted_iota(jnp.int32, shape, 0)
    lane = lax.broadcasted_iota(jnp.int32, shape, 1)
    col = jnp.bitwise_and(lane, rows - 1)
    start = place * rows
    low = (jnp.minimum(row, col) + start).astype(f32)
    high = (jnp.maximum(row, col) + start).astype(f32)
    own = (col + start).astype(f32)
    inner = scale_of(shape) * power(theta, high - low) * rest(theta, low + 1.0) * rest(theta, total - high)
    up = power(theta, (rows - col).astype(f32)) * rest(theta, own + 1.0)
    down = power(theta, (col + 1).astype(f32)) * rest(theta, total - own)
    full = jnp.where(row < rows, inner, jnp.where(row == rows, up, jnp.where(row == rows + 1, down, 0.0)))
    top = full.astype(bf16).astype(f32)
    gm[f] = jnp.where(lane >= 2 * rows, full - top, top).astype(bf16)

    shape = (rows, 128)
    theta = theta_of(shape)
    scale = scale_of(shape)
    row = lax.broadcasted_iota(jnp.int32, shape, 0)
    here = (row + start).astype(f32)
    tables[f, 0] = scale * power(theta, row.astype(f32)) * rest(theta, total - here)
    tables[f, 1] = scale * power(theta, (rows - 1 - row).astype(f32)) * rest(theta, here + 1.0)
    decay[f] = power(theta_of((8, 128)), float(rows))


def main_kernel(
    sizes, fields, viscous, e, tables, c_out,
    q, sp, xs, xr, zs, zr, ws, wr, gm, decay, carry, merged, speeds, stencil,
    in_sem, x_send, x_recv, z_send, z_recv, w_send, w_recv,
):
    px, py, pz = sizes
    nf, nx, ny, nz = q.shape
    blocks = nx // 32
    ix, iy, iz = lax.axis_index("gx"), lax.axis_index("gy"), lax.axis_index("gz")

    def x_at(k):
        return lax.rem(ix + k, px)

    z_up, z_down = lax.rem(iz + 1, pz), lax.rem(iz + pz - 1, pz)

    def load(f):
        return pltpu.make_async_copy(fields.at[f], q.at[f], in_sem.at[f])

    for f in range(nf):
        load(f).start()

    wr[...] = jnp.zeros_like(wr)
    barrier = pltpu.get_barrier_semaphore()
    for k in range(1, px):
        pl.semaphore_signal(barrier, inc=1, device_id={"gx": x_at(k)}, device_id_type=MESH)
    for to in (z_up, z_down):
        pl.semaphore_signal(barrier, inc=1, device_id={"gz": to}, device_id_type=MESH)
    for k in range(1, py):
        pl.semaphore_signal(barrier, inc=1, device_id={"gy": lax.rem(iy + k, py)}, device_id_type=MESH)

    def x_copy(f, k):
        return pltpu.make_async_remote_copy(
            src_ref=xs.at[f], dst_ref=xr.at[k - 1, f], send_sem=x_send.at[k - 1, f], recv_sem=x_recv.at[k - 1, f],
            device_id={"gx": x_at(k)}, device_id_type=MESH)

    def z_copy(f, side):
        return pltpu.make_async_remote_copy(
            src_ref=zs.at[side, f], dst_ref=zr.at[side, f], send_sem=z_send.at[side, f], recv_sem=z_recv.at[side, f],
            device_id={"gz": z_up if side == 0 else z_down}, device_id_type=MESH)

    def w_copy(f, side, k):
        to = lax.rem(iy + (k if side == 0 else py - k), py)
        return pltpu.make_async_remote_copy(
            src_ref=ws.at[side, f], dst_ref=wr.at[side, k - 1, f], send_sem=w_send.at[side, k - 1, f],
            recv_sem=w_recv.at[side, k - 1, f], device_id={"gy": to}, device_id_type=MESH)

    lane = lax.broadcasted_iota(jnp.int32, (ny, nz), 1)
    group = lax.shift_right_logical(lane, 2)
    zero = jnp.zeros((ny, nz), f32)

    def first_part(f, _):
        load(f).wait()

        def sums(t, state):
            fo, bo = state
            fo = ratio * (q[f, t] + fo)
            back = nx - 1 - t
            e[f, back] = bo
            bo = ratio * (q[f, back] + bo)
            return fo, bo

        fo, bo = lax.fori_loop(0, nx, sums, (zero, zero), unroll=4)
        xs[f, 0] = fo
        xs[f, 1] = q[f, nx - 1]
        xs[f, 2] = bo
        xs[f, 3] = q[f, 0]

        @pl.when(f == 0)
        def _():
            pl.semaphore_wait(barrier, px - 1 + 2 + py - 1)

        for k in range(1, px):
            x_copy(f, k).start()

        return 0

    lax.fori_loop(0, nf, first_part, 0)

    def pack_part(f, _):
        for g in range(blocks):
            def pack(t, state):
                last, lead = state
                turned = pltpu.roll(q[f, g * 32 + t], GROUP * t, 1)
                lead = jnp.where(group == t, turned, lead)
                last = jnp.where(group == jnp.bitwise_and(t + 31, 31), turned, last)
                return last, lead

            last, lead = lax.fori_loop(0, 32, pack, (zero, zero), unroll=4)
            zs[0, f, g] = last
            zs[1, f, g] = lead
        for side in range(2):
            z_copy(f, side).start()
        return 0

    lax.fori_loop(0, nf, pack_part, 0)

    def build(f, _):
        wall_tables(viscous[f], iy, ny, ny * py, gm, tables, decay, f)
        return 0

    lax.fori_loop(0, nf, build, 0)

    source = jnp.bitwise_and(lax.broadcasted_iota(jnp.int32, (2 * nz, nz), 0), nz - 1)
    target = lax.broadcasted_iota(jnp.int32, (2 * nz, nz), 1)
    reach = jnp.bitwise_and(source - target, nz - 1)
    weights = jnp.zeros((2 * nz, nz), f32)
    for k, c in ((1, 45.0), (2, -9.0), (3, 1.0)):
        weights = jnp.where(reach == k, c, jnp.where(reach == nz - k, -c, weights))
    stencil[...] = weights.astype(bf16)

    def scale_speeds(x, _):
        speeds[0, x] = (-advect * line_scale) * q[0, x]
        speeds[1, x] = (-advect / 60.0) * q[2, x]
        return 0

    lax.fori_loop(0, nx, scale_speeds, 0, unroll=4)

    def span_part(f):
        def some(t, _):
            here = q[f, pl.ds(t * SPAN_STEP, SPAN_STEP)].reshape(SPAN_STEP * ny, nz)
            top = here.astype(bf16)
            low = (here - top.astype(f32)).astype(bf16)
            both = jnp.concatenate([top, low], axis=1)
            made = jnp.dot(both, stencil[...], preferred_element_type=f32)
            sp[pl.ds(t * SPAN_STEP, SPAN_STEP)] = made.reshape(SPAN_STEP, ny, nz)
            return 0

        lax.fori_loop(0, nx // SPAN_STEP, some, 0)

    inside = jnp.bitwise_and(lane, 3)
    even = jnp.bitwise_and(group, 1) == 0
    edges = jnp.logical_or(group == 0, group == nz // GROUP - 1)
    closing = 1.0 / (1.0 - ratio ** (nx * px))

    def third_part(f, _):
        span_part(f)
        for side in range(2):
            z_copy(f, side).wait_recv()
        for g in range(blocks):
            left = zr[0, f, g] - zs[0, f, g]
            right = zr[1, f, g] - zs[1, f, g]
            low = (
                jnp.where(inside == 0, -45.0 * pltpu.roll(left, nz - 3, 1), 0.0)
                + jnp.where(inside <= 1, 9.0 * pltpu.roll(left, nz - 2, 1), 0.0)
                - jnp.where(inside <= 2, pltpu.roll(left, nz - 1, 1), 0.0)
            )
            high = (
                jnp.where(inside == 3, 45.0 * pltpu.roll(right, 3, 1), 0.0)
                - jnp.where(inside >= 2, 9.0 * pltpu.roll(right, 2, 1), 0.0)
                + jnp.where(inside >= 1, pltpu.roll(right, 1, 1), 0.0)
            )
            low = pltpu.roll(low, GROUP, 1)
            high = pltpu.roll(high, nz - GROUP, 1)
            merged[g, 0] = jnp.where(even, low, high)
            merged[g, 1] = jnp.where(even, high, low)

        for k in range(1, px):
            x_copy(f, k).wait_recv()
        ahead = ratio ** (nx * (px - 1)) * xs[f, 0]
        behind = ratio ** (nx * (px - 1)) * xs[f, 2]
        for k in range(1, px):
            ahead = ahead + ratio ** (nx * (k - 1)) * xr[k - 1, f, 0]
            behind = behind + ratio ** (nx * (k - 1)) * xr[px - k - 1, f, 2]
        carry[0] = closing * behind
        matrix = gm[f]
        end = xr[px - 2, f, 3]

        def some(t, state):
            forward, previous, bw = state
            base = t * STEP
            block = base // 32
            place = base - block * 32
            tops, lows = [], []
            for o in range(STEP):
                x = base + o
                here = q[f, x]
                if o < STEP - 1:
                    after = q[f, x + 1]
                else:
                    after = jnp.where(x == nx - 1, end, q[f, jnp.minimum(x + 1, nx - 1)])
                turn = jnp.bitwise_and(nz - GROUP * (place + o), nz - 1)
                span = sp[x] + jnp.where(edges, pltpu.roll(merged[block, o % 2], turn, 1), 0.0)
                slope = (e[f, x] - forward) + bw * carry[0] + (near_scale / line_scale) * (after - previous)
                whole = here + speeds[0, x] * slope + speeds[1, x] * span
                top = whole.astype(bf16)
                tops.append(top)
                lows.append((whole - top.astype(f32)).astype(bf16))
                forward = ratio * (here + forward)
                previous = here
                bw = bw * (1.0 / ratio)
            top = jnp.concatenate(tops, axis=1)
            right = jnp.concatenate([top, jnp.concatenate(lows, axis=1), top], axis=0)
            solved = jnp.dot(matrix, right, preferred_element_type=f32)
            for o in range(STEP):
                e[f, base + o] = solved[:ny, o * nz : (o + 1) * nz]
                ws[0, f, pl.ds(base + o, 1), :] = solved[ny : ny + 1, o * nz : (o + 1) * nz]
                ws[1, f, pl.ds(base + o, 1), :] = solved[ny + 1 : ny + 2, o * nz : (o + 1) * nz]
            return forward, previous, bw

        lax.fori_loop(0, nx // STEP, some, (closing * ahead, xr[0, f, 1], f32(ratio ** (nx - 1))))

        for k in range(1, py):
            @pl.when(iy + k < py)
            def _():
                w_copy(f, 0, k).start()

            @pl.when(iy >= k)
            def _():
                w_copy(f, 1, k).start()
        return 0

    lax.fori_loop(0, nf, third_part, 0)

    def fourth_part(f, _):
        for k in range(1, py):
            @pl.when(iy >= k)
            def _():
                w_copy(f, 0, k).wait_recv()

            @pl.when(iy + k < py)
            def _():
                w_copy(f, 1, k).wait_recv()
        step = jnp.broadcast_to(decay[f][0:1, :], (nx, nz))
        for side in range(2):
            total = wr[side, py - 2, f]
            for k in range(py - 2, 0, -1):
                total = wr[side, k - 1, f] + step * total
            c_out[side, f] = total
        return 0

    lax.fori_loop(0, nf, fourth_part, 0)

    def finish(f, _):
        for k in range(1, px):
            x_copy(f, k).wait_send()
        for side in range(2):
            z_copy(f, side).wait_send()
        for k in range(1, py):
            @pl.when(iy + k < py)
            def _():
                w_copy(f, 0, k).wait_send()

            @pl.when(iy >= k)
            def _():
                w_copy(f, 1, k).wait_send()
        return 0

    lax.fori_loop(0, nf, finish, 0)


def last_kernel(v, tables, rows, out, made, sem):
    nf, nx = v.shape[:2]
    parts = nx // PART

    def copy(t):
        f, x = t // parts, (t % parts) * PART
        return pltpu.make_async_copy(made.at[f, pl.ds(x, PART)], out.at[f, pl.ds(x, PART)], sem.at[t])

    def some(t, _):
        f, x = t // parts, (t % parts) * PART
        up, down = tables[f, 0], tables[f, 1]
        for o in range(PART):
            made[f, x + o] = v[f, x + o] + up * rows[0, f, pl.ds(x + o, 1), :] + down * rows[1, f, pl.ds(x + o, 1), :]
        copy(t).start()
        return 0

    lax.fori_loop(0, nf * parts, some, 0)

    def finish(t, _):
        copy(t).wait()
        return 0

    lax.fori_loop(0, nf * parts, finish, 0)


def shards(fields, viscous):
    nf, nx, ny, nz = fields.shape
    px, py, pz = (lax.axis_size(a) for a in ("gx", "gy", "gz"))
    blocks = nx // 32
    in_vmem = pl.BlockSpec(memory_space=pltpu.VMEM)
    size = 4 * nf * nx * ny * nz
    any_space = pl.BlockSpec(memory_space=pl.ANY)
    v, tables, rows = pl.pallas_call(
        functools.partial(main_kernel, (px, py, pz)),
        out_shape=(
            jax.ShapeDtypeStruct((nf, nx, ny, nz), f32),
            jax.ShapeDtypeStruct((nf, 2, ny, nz), f32),
            jax.ShapeDtypeStruct((2, nf, nx, nz), f32),
        ),
        in_specs=[pl.BlockSpec(memory_space=pltpu.HBM), pl.BlockSpec(memory_space=pltpu.SMEM)],
        out_specs=(in_vmem, in_vmem, in_vmem),
        scratch_shapes=[
            pltpu.VMEM((nf, nx, ny, nz), f32),
            pltpu.VMEM((nx, ny, nz), f32),
            pltpu.VMEM((nf, 4, ny, nz), f32),
            pltpu.VMEM((px - 1, nf, 4, ny, nz), f32),
            pltpu.VMEM((2, nf, blocks, ny, nz), f32),
            pltpu.VMEM((2, nf, blocks, ny, nz), f32),
            pltpu.VMEM((2, nf, nx, nz), f32),
            pltpu.VMEM((2, py - 1, nf, nx, nz), f32),
            pltpu.VMEM((nf, ny + 16, 3 * ny), bf16),
            pltpu.VMEM((nf, 8, nz), f32),
            pltpu.VMEM((2, ny, nz), f32),
            pltpu.VMEM((blocks, 2, ny, nz), f32),
            pltpu.VMEM((2, nx, ny, nz), f32),
            pltpu.VMEM((2 * nz, nz), bf16),
            pltpu.SemaphoreType.DMA((nf,)),
            pltpu.SemaphoreType.DMA((px - 1, nf)),
            pltpu.SemaphoreType.DMA((px - 1, nf)),
            pltpu.SemaphoreType.DMA((2, nf)),
            pltpu.SemaphoreType.DMA((2, nf)),
            pltpu.SemaphoreType.DMA((2, py - 1, nf)),
            pltpu.SemaphoreType.DMA((2, py - 1, nf)),
        ],
        compiler_params=pltpu.CompilerParams(
            collective_id=0, has_side_effects=True, vmem_limit_bytes=min(5 * size, 56 << 20)
        ),
        name="section",
    )(fields, viscous)
    return pl.pallas_call(
        last_kernel,
        out_shape=jax.ShapeDtypeStruct((nf, nx, ny, nz), f32),
        in_specs=[in_vmem, in_vmem, in_vmem],
        out_specs=any_space,
        scratch_shapes=[
            pltpu.VMEM((nf, nx, ny, nz), f32),
            pltpu.SemaphoreType.DMA((nf * (nx // PART),)),
        ],
        compiler_params=pltpu.CompilerParams(vmem_limit_bytes=min(3 * size, 48 << 20)),
        name="carried",
    )(v, tables, rows)


def solution(mesh):
    in_specs = (P(None, "gx", "gy", "gz"), P())
    out_specs = P(None, "gx", "gy", "gz")
    return jax.shard_map(shards, mesh=mesh, in_specs=in_specs, out_specs=out_specs, check_vma=False)
```

```python
import functools
import math

import jax
import jax.numpy as jnp
from jax import lax
from jax.experimental import pallas as pl
from jax.experimental.pallas import tpu as pltpu
from jax.sharding import PartitionSpec as P

advect = 0.3
ratio = (-1.0 + math.sqrt(5.0) / 3.0) * 1.5
line_scale = -25.0 / 12.0
near_scale = 1.0 / 12.0
MESH = pl.DeviceIdType.MESH
f32 = jnp.float32
bf16 = jnp.bfloat16
GROUP = 4
STEP = 16
SPAN_STEP = 16
PART = 8


def power(theta, count):
    return jnp.exp(-theta * count)


def rest(theta, count):
    return 1.0 - jnp.exp(-2.0 * theta * count)


def wall_tables(nu, place, rows, total, gm, tables, decay, f):
    shape = (rows + 16, 3 * rows)

    def theta_of(shape):
        half = 0.5 * lax.rsqrt(jnp.full(shape, nu, f32))
        return 2.0 * jnp.log(half + jnp.sqrt(1.0 + half * half))

    def scale_of(shape):
        theta = theta_of(shape)
        return power(theta, 1.0) / (nu * rest(theta, 1.0) * rest(theta, total + 1.0))

    theta = theta_of(shape)
    row = lax.broadcasted_iota(jnp.int32, shape, 0)
    lane = lax.broadcasted_iota(jnp.int32, shape, 1)
    col = jnp.bitwise_and(lane, rows - 1)
    start = place * rows
    low = (jnp.minimum(row, col) + start).astype(f32)
    high = (jnp.maximum(row, col) + start).astype(f32)
    own = (col + start).astype(f32)
    inner = scale_of(shape) * power(theta, high - low) * rest(theta, low + 1.0) * rest(theta, total - high)
    up = power(theta, (rows - col).astype(f32)) * rest(theta, own + 1.0)
    down = power(theta, (col + 1).astype(f32)) * rest(theta, total - own)
    full = jnp.where(row < rows, inner, jnp.where(row == rows, up, jnp.where(row == rows + 1, down, 0.0)))
    top = full.astype(bf16).astype(f32)
    gm[f] = jnp.where(lane >= 2 * rows, full - top, top).astype(bf16)

    shape = (rows, 128)
    theta = theta_of(shape)
    scale = scale_of(shape)
    row = lax.broadcasted_iota(jnp.int32, shape, 0)
    here = (row + start).astype(f32)
    tables[f, 0] = scale * power(theta, row.astype(f32)) * rest(theta, total - here)
    tables[f, 1] = scale * power(theta, (rows - 1 - row).astype(f32)) * rest(theta, here + 1.0)
    decay[f] = power(theta_of((8, 128)), float(rows))


def main_kernel(
    sizes, fields, viscous, e, tables, c_out,
    q, sp, xs, xr, zs, zr, ws, wr, gm, decay, carry, merged, speeds, stencil,
    in_sem, x_send, x_recv, z_send, z_recv, w_send, w_recv,
):
    px, py, pz = sizes
    nf, nx, ny, nz = q.shape
    blocks = nx // 32
    ix, iy, iz = lax.axis_index("gx"), lax.axis_index("gy"), lax.axis_index("gz")

    def x_at(k):
        return lax.rem(ix + k, px)

    z_up, z_down = lax.rem(iz + 1, pz), lax.rem(iz + pz - 1, pz)

    def load(f):
        return pltpu.make_async_copy(fields.at[f], q.at[f], in_sem.at[f])

    for f in range(nf):
        load(f).start()

    wr[...] = jnp.zeros_like(wr)
    barrier = pltpu.get_barrier_semaphore()
    for k in range(1, px):
        pl.semaphore_signal(barrier, inc=1, device_id={"gx": x_at(k)}, device_id_type=MESH)
    for to in (z_up, z_down):
        pl.semaphore_signal(barrier, inc=1, device_id={"gz": to}, device_id_type=MESH)
    for k in range(1, py):
        pl.semaphore_signal(barrier, inc=1, device_id={"gy": lax.rem(iy + k, py)}, device_id_type=MESH)

    def x_copy(f, k):
        return pltpu.make_async_remote_copy(
            src_ref=xs.at[f], dst_ref=xr.at[k - 1, f], send_sem=x_send.at[k - 1, f], recv_sem=x_recv.at[k - 1, f],
            device_id={"gx": x_at(k)}, device_id_type=MESH)

    def z_copy(f, side):
        return pltpu.make_async_remote_copy(
            src_ref=zs.at[side, f], dst_ref=zr.at[side, f], send_sem=z_send.at[side, f], recv_sem=z_recv.at[side, f],
            device_id={"gz": z_up if side == 0 else z_down}, device_id_type=MESH)

    def w_copy(f, side, k):
        to = lax.rem(iy + (k if side == 0 else py - k), py)
        return pltpu.make_async_remote_copy(
            src_ref=ws.at[side, f], dst_ref=wr.at[side, k - 1, f], send_sem=w_send.at[side, k - 1, f],
            recv_sem=w_recv.at[side, k - 1, f], device_id={"gy": to}, device_id_type=MESH)

    lane = lax.broadcasted_iota(jnp.int32, (ny, nz), 1)
    group = lax.shift_right_logical(lane, 2)
    zero = jnp.zeros((ny, nz), f32)

    def first_part(f, _):
        load(f).wait()

        def sums(t, state):
            fo, bo = state
            fo = ratio * (q[f, t] + fo)
            back = nx - 1 - t
            e[f, back] = bo
            bo = ratio * (q[f, back] + bo)
            return fo, bo

        fo, bo = lax.fori_loop(0, nx, sums, (zero, zero), unroll=8)
        xs[f, 0] = fo
        xs[f, 1] = q[f, nx - 1]
        xs[f, 2] = bo
        xs[f, 3] = q[f, 0]

        @pl.when(f == 0)
        def _():
            pl.semaphore_wait(barrier, px - 1 + 2 + py - 1)

        for k in range(1, px):
            x_copy(f, k).start()

        return 0

    lax.fori_loop(0, nf, first_part, 0)

    def pack_part(f, _):
        for g in range(blocks):
            def pack(t, state):
                last, lead = state
                turned = pltpu.roll(q[f, g * 32 + t], GROUP * t, 1)
                lead = jnp.where(group == t, turned, lead)
                last = jnp.where(group == jnp.bitwise_and(t + 31, 31), turned, last)
                return last, lead

            last, lead = lax.fori_loop(0, 32, pack, (zero, zero), unroll=8)
            zs[0, f, g] = last
            zs[1, f, g] = lead
        for side in range(2):
            z_copy(f, side).start()
        return 0

    lax.fori_loop(0, nf, pack_part, 0)

    def build(f, _):
        wall_tables(viscous[f], iy, ny, ny * py, gm, tables, decay, f)
        return 0

    lax.fori_loop(0, nf, build, 0)

    source = jnp.bitwise_and(lax.broadcasted_iota(jnp.int32, (2 * nz, nz), 0), nz - 1)
    target = lax.broadcasted_iota(jnp.int32, (2 * nz, nz), 1)
    reach = jnp.bitwise_and(source - target, nz - 1)
    weights = jnp.zeros((2 * nz, nz), f32)
    for k, c in ((1, 45.0), (2, -9.0), (3, 1.0)):
        weights = jnp.where(reach == k, c, jnp.where(reach == nz - k, -c, weights))
    stencil[...] = weights.astype(bf16)

    def scale_speeds(x, _):
        speeds[0, x] = (-advect * line_scale) * q[0, x]
        speeds[1, x] = (-advect / 60.0) * q[2, x]
        return 0

    lax.fori_loop(0, nx, scale_speeds, 0, unroll=4)

    def span_part(f):
        def some(t, _):
            here = q[f, pl.ds(t * SPAN_STEP, SPAN_STEP)].reshape(SPAN_STEP * ny, nz)
            top = here.astype(bf16)
            low = (here - top.astype(f32)).astype(bf16)
            both = jnp.concatenate([top, low], axis=1)
            made = jnp.dot(both, stencil[...], preferred_element_type=f32)
            sp[pl.ds(t * SPAN_STEP, SPAN_STEP)] = made.reshape(SPAN_STEP, ny, nz)
            return 0

        lax.fori_loop(0, nx // SPAN_STEP, some, 0)

    inside = jnp.bitwise_and(lane, 3)
    even = jnp.bitwise_and(group, 1) == 0
    edges = jnp.logical_or(group == 0, group == nz // GROUP - 1)
    closing = 1.0 / (1.0 - ratio ** (nx * px))

    def third_part(f, _):
        span_part(f)
        for side in range(2):
            z_copy(f, side).wait_recv()
        for g in range(blocks):
            left = zr[0, f, g] - zs[0, f, g]
            right = zr[1, f, g] - zs[1, f, g]
            low = (
                jnp.where(inside == 0, -45.0 * pltpu.roll(left, nz - 3, 1), 0.0)
                + jnp.where(inside <= 1, 9.0 * pltpu.roll(left, nz - 2, 1), 0.0)
                - jnp.where(inside <= 2, pltpu.roll(left, nz - 1, 1), 0.0)
            )
            high = (
                jnp.where(inside == 3, 45.0 * pltpu.roll(right, 3, 1), 0.0)
                - jnp.where(inside >= 2, 9.0 * pltpu.roll(right, 2, 1), 0.0)
                + jnp.where(inside >= 1, pltpu.roll(right, 1, 1), 0.0)
            )
            low = pltpu.roll(low, GROUP, 1)
            high = pltpu.roll(high, nz - GROUP, 1)
            merged[g, 0] = jnp.where(even, low, high)
            merged[g, 1] = jnp.where(even, high, low)

        for k in range(1, px):
            x_copy(f, k).wait_recv()
        ahead = ratio ** (nx * (px - 1)) * xs[f, 0]
        behind = ratio ** (nx * (px - 1)) * xs[f, 2]
        for k in range(1, px):
            ahead = ahead + ratio ** (nx * (k - 1)) * xr[k - 1, f, 0]
            behind = behind + ratio ** (nx * (k - 1)) * xr[px - k - 1, f, 2]
        carry[0] = closing * behind
        matrix = gm[f]
        end = xr[px - 2, f, 3]

        def some(t, state):
            forward, previous, bw = state
            base = t * STEP
            block = base // 32
            place = base - block * 32
            tops, lows = [], []
            for o in range(STEP):
                x = base + o
                here = q[f, x]
                if o < STEP - 1:
                    after = q[f, x + 1]
                else:
                    after = jnp.where(x == nx - 1, end, q[f, jnp.minimum(x + 1, nx - 1)])
                turn = jnp.bitwise_and(nz - GROUP * (place + o), nz - 1)
                span = sp[x] + jnp.where(edges, pltpu.roll(merged[block, o % 2], turn, 1), 0.0)
                slope = (e[f, x] - forward) + bw * carry[0] + (near_scale / line_scale) * (after - previous)
                whole = here + speeds[0, x] * slope + speeds[1, x] * span
                top = whole.astype(bf16)
                tops.append(top)
                lows.append((whole - top.astype(f32)).astype(bf16))
                forward = ratio * (here + forward)
                previous = here
                bw = bw * (1.0 / ratio)
            top = jnp.concatenate(tops, axis=1)
            right = jnp.concatenate([top, jnp.concatenate(lows, axis=1), top], axis=0)
            solved = jnp.dot(matrix, right, preferred_element_type=f32)
            for o in range(STEP):
                e[f, base + o] = solved[:ny, o * nz : (o + 1) * nz]
                ws[0, f, pl.ds(base + o, 1), :] = solved[ny : ny + 1, o * nz : (o + 1) * nz]
                ws[1, f, pl.ds(base + o, 1), :] = solved[ny + 1 : ny + 2, o * nz : (o + 1) * nz]
            return forward, previous, bw

        lax.fori_loop(0, nx // STEP, some, (closing * ahead, xr[0, f, 1], f32(ratio ** (nx - 1))))

        for k in range(1, py):
            @pl.when(iy + k < py)
            def _():
                w_copy(f, 0, k).start()

            @pl.when(iy >= k)
            def _():
                w_copy(f, 1, k).start()
        return 0

    lax.fori_loop(0, nf, third_part, 0)

    def fourth_part(f, _):
        for k in range(1, py):
            @pl.when(iy >= k)
            def _():
                w_copy(f, 0, k).wait_recv()

            @pl.when(iy + k < py)
            def _():
                w_copy(f, 1, k).wait_recv()
        step = jnp.broadcast_to(decay[f][0:1, :], (nx, nz))
        for side in range(2):
            total = wr[side, py - 2, f]
            for k in range(py - 2, 0, -1):
                total = wr[side, k - 1, f] + step * total
            c_out[side, f] = total
        return 0

    lax.fori_loop(0, nf, fourth_part, 0)

    def finish(f, _):
        for k in range(1, px):
            x_copy(f, k).wait_send()
        for side in range(2):
            z_copy(f, side).wait_send()
        for k in range(1, py):
            @pl.when(iy + k < py)
            def _():
                w_copy(f, 0, k).wait_send()

            @pl.when(iy >= k)
            def _():
                w_copy(f, 1, k).wait_send()
        return 0

    lax.fori_loop(0, nf, finish, 0)


def last_kernel(v, tables, rows, out, made, sem):
    nf, nx = v.shape[:2]
    parts = nx // PART

    def copy(t):
        f, x = t // parts, (t % parts) * PART
        return pltpu.make_async_copy(made.at[f, pl.ds(x, PART)], out.at[f, pl.ds(x, PART)], sem.at[t])

    def some(t, _):
        f, x = t // parts, (t % parts) * PART
        up, down = tables[f, 0], tables[f, 1]
        for o in range(PART):
            made[f, x + o] = v[f, x + o] + up * rows[0, f, pl.ds(x + o, 1), :] + down * rows[1, f, pl.ds(x + o, 1), :]
        copy(t).start()
        return 0

    lax.fori_loop(0, nf * parts, some, 0)

    def finish(t, _):
        copy(t).wait()
        return 0

    lax.fori_loop(0, nf * parts, finish, 0)


def shards(fields, viscous):
    nf, nx, ny, nz = fields.shape
    px, py, pz = (lax.axis_size(a) for a in ("gx", "gy", "gz"))
    blocks = nx // 32
    in_vmem = pl.BlockSpec(memory_space=pltpu.VMEM)
    size = 4 * nf * nx * ny * nz
    any_space = pl.BlockSpec(memory_space=pl.ANY)
    v, tables, rows = pl.pallas_call(
        functools.partial(main_kernel, (px, py, pz)),
        out_shape=(
            jax.ShapeDtypeStruct((nf, nx, ny, nz), f32),
            jax.ShapeDtypeStruct((nf, 2, ny, nz), f32),
            jax.ShapeDtypeStruct((2, nf, nx, nz), f32),
        ),
        in_specs=[pl.BlockSpec(memory_space=pltpu.HBM), pl.BlockSpec(memory_space=pltpu.SMEM)],
        out_specs=(in_vmem, in_vmem, in_vmem),
        scratch_shapes=[
            pltpu.VMEM((nf, nx, ny, nz), f32),
            pltpu.VMEM((nx, ny, nz), f32),
            pltpu.VMEM((nf, 4, ny, nz), f32),
            pltpu.VMEM((px - 1, nf, 4, ny, nz), f32),
            pltpu.VMEM((2, nf, blocks, ny, nz), f32),
            pltpu.VMEM((2, nf, blocks, ny, nz), f32),
            pltpu.VMEM((2, nf, nx, nz), f32),
            pltpu.VMEM((2, py - 1, nf, nx, nz), f32),
            pltpu.VMEM((nf, ny + 16, 3 * ny), bf16),
            pltpu.VMEM((nf, 8, nz), f32),
            pltpu.VMEM((2, ny, nz), f32),
            pltpu.VMEM((blocks, 2, ny, nz), f32),
            pltpu.VMEM((2, nx, ny, nz), f32),
            pltpu.VMEM((2 * nz, nz), bf16),
            pltpu.SemaphoreType.DMA((nf,)),
            pltpu.SemaphoreType.DMA((px - 1, nf)),
            pltpu.SemaphoreType.DMA((px - 1, nf)),
            pltpu.SemaphoreType.DMA((2, nf)),
            pltpu.SemaphoreType.DMA((2, nf)),
            pltpu.SemaphoreType.DMA((2, py - 1, nf)),
            pltpu.SemaphoreType.DMA((2, py - 1, nf)),
        ],
        compiler_params=pltpu.CompilerParams(
            collective_id=0, has_side_effects=True, vmem_limit_bytes=47 << 20
        ),
        name="section",
    )(fields, viscous)
    return pl.pallas_call(
        last_kernel,
        out_shape=jax.ShapeDtypeStruct((nf, nx, ny, nz), f32),
        in_specs=[in_vmem, in_vmem, in_vmem],
        out_specs=any_space,
        scratch_shapes=[
            pltpu.VMEM((nf, nx, ny, nz), f32),
            pltpu.SemaphoreType.DMA((nf * (nx // PART),)),
        ],
        compiler_params=pltpu.CompilerParams(vmem_limit_bytes=min(3 * size, 48 << 20)),
        name="carried",
    )(v, tables, rows)


def solution(mesh):
    in_specs = (P(None, "gx", "gy", "gz"), P())
    out_specs = P(None, "gx", "gy", "gz")
    return jax.shard_map(shards, mesh=mesh, in_specs=in_specs, out_specs=out_specs, check_vma=False)
```
